512 devices in a mesh: lat: 128 (over z_lo, x, y, core), coh: 4 (over z_hi).
Axes of the slice: x: 4, y: 4, z: 16 (z_hi: 4, z_lo: 4; z = z_hi * 4 + z_lo), core: 2. Of those that a mesh axis runs over, the one named last changes fastest.
Arguments:
- density: float32 [64, 1024, 4096], P('coh', 'lat'), may hold values from 0.1 to 2
- forage: float32 [6, 1024, 4096], P(None, 'lat'), may hold values from 0.1 to 3
- access: float32 [64, 6], P('coh'), may hold values from -3 to 3
- mortality: float32 [64], P('coh'), may hold values from 0.02 to 0.5
- maturity: float32 [64], P('coh'), may hold values from 0 to 1
- recruit_rate: float32 [1024, 4096], P('lat'), may hold values from 0.2 to 2
- zonal_inverse: float32 [64, 128, 128], P('coh'), may hold values from 0 to 0.8, as said below
- diffusivity: float32 [1024, 4096], P('lat'), may hold values from 0.05 to 0.2
- drift: float32 [1024, 4096], P('lat'), may hold values from -0.1 to 0.1
- land_mask: int32 [1024, 4096], P('lat'), may hold values 0 or 1
- effort: float32 [1024, 4096], P('lat'), may hold values from 0.02 to 3, as said below
- strata_map: int32 [1024, 4096], P('lat'), may hold values from 0 to 24, as said below
- length_bin: int32 [64], P('coh'), may hold values from 0 to 31
- selectivity: float32 [32], replicated, may hold values from 0.2 to 1
Outputs:
- new_density: float32 [64, 1024, 4096], P('coh', 'lat')
- catch_table: float32 [25, 32], replicated
The draws below stay inside these ranges and needn't reach their ends.
Inputs may be any that keep to these rules, and one draw needn't show every extreme that they name: `zonal_inverse`: dominant diagonal, nonnegative entries. `effort`: Positive. `strata_map`: every stratum has cells.
All inputs are finite; a program needn't handle non-finite values. No bound on the sum of `land_mask` on one device may be relied on, other than what follows from the above.
Results may differ from the reference program's by a relative error of at most 0.0003.
Values sent between devices are 32-bit elements; how exact they have to be, the bound alone decides.
No kernel may reach another device: no remote copies, remote signals or barrier semaphores. Data moves between devices by JAX's collectives and lax.ppermute only.
A program may use at most 128 MiB of HBM per device.

```python
import math
import jax
import jax.numpy as jnp
from jax import lax

LON = 4096
FORAGE = 6
STRATA = 25
NLEN = 32
BLK = 128
SWEEPS = 8
LAT = 1024
COHORTS = 64


def draw_zonal_inverse(key, part):
    key = jax.random.fold_in(key, 11)
    first_key, second_key = jax.random.split(key)
    identity = jnp.eye(BLK, dtype=jnp.float32)
    diagonal = jax.random.uniform(first_key, (COHORTS, BLK, 1), jnp.float32, 0.5, 0.8)
    offdiag = jax.random.uniform(second_key, (COHORTS, BLK, BLK), jnp.float32, 0.0, 0.003)
    return identity * diagonal + (1.0 - identity) * offdiag


def draw_effort(key, part):
    key = jax.random.fold_in(key, 12)
    rows = jnp.arange(LAT, dtype=jnp.float32)[:, None]
    slope = 1.0 + 2.0 * rows / max(LAT - 1, 1)
    base = jax.random.uniform(key, (LAT, LON), jnp.float32, 0.2, 1.0)
    return base * slope


def draw_strata_map(key, part):
    key = jax.random.fold_in(key, 13)
    reach = LON // 32
    jitter = jax.random.randint(key, (LAT, 1), -reach, reach + 1, jnp.int32)
    columns = jnp.arange(LON, dtype=jnp.int32)[None, :] + jitter
    lon_band = jnp.clip(columns * 5 // LON, 0, 4)
    lat_band = jnp.arange(LAT, dtype=jnp.int32)[:, None] * 5 // LAT
    return (lat_band * 5 + lon_band).astype(jnp.int32)


def place_ends(drawn, stream_key, least, largest):
    longest = drawn.shape.index(max(drawn.shape))
    spots = []
    for shift in (0, 1):
        where = [jax.random.randint(jax.random.fold_in(stream_key, axis), (), 0, length) for axis, length in enumerate(drawn.shape)]
        where[longest] = (where[longest] + shift) % drawn.shape[longest]
        spots.append(tuple(where))
    return drawn.at[spots[0]].set(least).at[spots[1]].set(largest)


def shard_levels(key, shape, pieces, least, top_value):
    gain, own = 1.0, jax.random.fold_in(key, 6)
    for position, shards_of in pieces:
        draws = jnp.exp(jax.random.uniform(jax.random.fold_in(own, position), (shards_of,), jnp.float32, least / len(pieces), top_value / len(pieces)))
        gain = gain * jnp.repeat(draws, shape[position] // shards_of).reshape([-1 if axis == position else 1 for axis in range(len(shape))])
    return gain


def gaussian(key, dims, width, most, pieces=(), held_as=jnp.bfloat16):
    drawn = width * jax.random.normal(key, dims, jnp.float32)
    if pieces:
        drawn = drawn * shard_levels(key, dims, pieces, -0.22, 0.18)
    return jnp.clip(drawn, -most, most).astype(held_as)


def setup_inputs(seed: int = 0) -> dict:
    key_of = jax.random.split(jax.random.key(seed), 15)
    return {
        "density": jnp.clip(jnp.exp(math.log(2.0) - 2.9957323 * jax.random.uniform(key_of[0], (COHORTS, LAT, LON), jnp.float32) ** shard_levels(key_of[0], (COHORTS, LAT, LON), ((0, 4), (1, 128)), -0.2, 0.2)), 0.1, 2.0),
        "forage": jnp.clip(jnp.exp(math.log(3.0) - 3.4011974 * jax.random.uniform(key_of[1], (FORAGE, LAT, LON), jnp.float32) ** shard_levels(key_of[1], (FORAGE, LAT, LON), ((1, 128),), -0.2, 0.2)), 0.1, 3.0),
        "access": gaussian(key_of[2], (COHORTS, FORAGE), 0.5, 3.0, ((0, 4),), jnp.float32),
        "mortality": jnp.clip(jnp.exp(math.log(0.5) - 3.218876 * jax.random.uniform(key_of[3], (COHORTS,), jnp.float32) ** shard_levels(key_of[3], (COHORTS,), ((0, 4),), -0.2, 0.2)), 0.02, 0.5),
        "maturity": jnp.clip(1.0 * jax.random.uniform(key_of[4], (COHORTS,), jnp.float32) ** shard_levels(key_of[4], (COHORTS,), ((0, 4),), -0.2, 0.2), 0.0, 1.0),
        "recruit_rate": jnp.clip(jnp.exp(math.log(2.0) - 2.3025851 * jax.random.uniform(key_of[5], (LAT, LON), jnp.float32) ** shard_levels(key_of[5], (LAT, LON), ((0, 128),), -0.2, 0.2)), 0.2, 2.0),
        "zonal_inverse": draw_zonal_inverse(jax.random.fold_in(key_of[14], 71), 0),
        "diffusivity": jnp.clip(0.05 + 0.15 * jax.random.uniform(key_of[7], (LAT, LON), jnp.float32) ** shard_levels(key_of[7], (LAT, LON), ((0, 128),), -0.2, 0.2), 0.05, 0.2),
        "drift": jnp.clip(jax.random.uniform(key_of[8], (LAT, LON), jnp.float32, -0.1, 0.1) * shard_levels(key_of[8], (LAT, LON), ((0, 128),), -0.4, 0.0), -0.1, 0.1),
        "land_mask": place_ends((jax.random.randint(key_of[9], (LAT, LON), 0, 5) < 4).astype(jnp.int32), jax.random.fold_in(key_of[9], 1), 0, 1),
        "effort": draw_effort(jax.random.fold_in(key_of[14], 71), 0),
        "strata_map": draw_strata_map(jax.random.fold_in(key_of[14], 71), 0),
        "length_bin": place_ends(jax.random.randint(key_of[12], (COHORTS,), 0, NLEN), jax.random.fold_in(key_of[12], 1), 0, NLEN - 1).astype(jnp.int32),
        "selectivity": jnp.clip(jnp.exp(jax.random.uniform(key_of[13], (NLEN,), jnp.float32, math.log(0.2), math.log(1.0))), 0.2, 1.0),
    }


def zonal_apply(field, inverse):
    blocks = field.reshape(LAT, LON // BLK, BLK)
    return jnp.einsum('rbk,jk->rbj', blocks, inverse, precision=lax.Precision.HIGHEST).reshape(LAT, LON)


def meridional(zonal, diffusivity, drift, ocean_mask):
    padded = jnp.pad(zonal, ((1, 1), (0, 0)))
    north_rows = padded[2:]
    south_rows = padded[:-2]
    return ocean_mask * (zonal + diffusivity * (north_rows - 2.0 * zonal + south_rows) - drift * (north_rows - south_rows) * 0.5)


def reference(density, forage, access, mortality, maturity, recruit_rate, zonal_inverse, diffusivity, drift, land_mask, effort, strata_map, length_bin, selectivity):
    ocean_mask = land_mask.astype(jnp.float32)
    spawning = jnp.einsum('c,crl->rl', maturity, density, precision=lax.Precision.HIGHEST)
    recruits = recruit_rate * spawning / (1.0 + spawning / 16.0)
    aged_fields = jnp.concatenate([recruits[None], density[:-2], (density[-2] + density[-1])[None]], axis=0)
    strata_hot = (strata_map[None] == jnp.arange(STRATA, dtype=jnp.int32)[:, None, None]).astype(jnp.float32)

    def one_cohort(items):
        aged, weights, rate, inverse = items
        habitat = jax.nn.sigmoid(jnp.einsum('g,grl->rl', weights, forage, precision=lax.Precision.HIGHEST))
        field = aged * jnp.exp(-rate) * (0.5 + habitat) * ocean_mask
        for sweep in range(SWEEPS):
            field = meridional(zonal_apply(field, inverse), diffusivity, drift, ocean_mask)
        totals = jnp.einsum('rl,srl->s', effort * field, strata_hot, precision=lax.Precision.HIGHEST)
        return field, totals

    new_density, totals = lax.map(one_cohort, (aged_fields, access, mortality, zonal_inverse))
    length_hot = (length_bin[:, None] == jnp.arange(NLEN, dtype=jnp.int32)[None, :]).astype(jnp.float32)
    cohort_select = jnp.dot(length_hot, selectivity, precision=lax.Precision.HIGHEST)
    catch_table = jnp.einsum('cs,cl->sl', totals * cohort_select[:, None], length_hot, precision=lax.Precision.HIGHEST)
    catch_table = catch_table * (25.0 / (LAT * LON))
    return new_density, catch_table
```

```python
import jax
import jax.numpy as jnp
from jax import lax
from jax.experimental import pallas as pl
from jax.experimental.pallas import tpu as pltpu
from jax.sharding import Mesh, PartitionSpec as P

STRATA = 25
NLEN = 32
BLK = 128
SWEEPS = 8
LAT = ("zl", "x", "y", "core")
COH = "zh"
AXES = (("zl", 4), ("x", 4), ("y", 4), ("core", 2), ("zh", 4))
ROWS = 8
NB = 32
BAND = ROWS * NB
SPAD = 32
PARTS = 4
PART = BAND // PARTS
STEP = 2


def split16(x):
    hi = x.astype(jnp.bfloat16)
    lo = (x - hi.astype(jnp.float32)).astype(jnp.bfloat16)
    return hi, lo


def start_kernel(flag, access_in, mortality_in, maturity_in, density, forage, land, diffusivity, drift, head, tail, gain0, spawn, dens, fora, ocean, diff, drif, access, mortality, maturity, sems, small_sems):
    last = mortality.shape[0] - 1
    cut = head.shape[0] - 2
    pairs = ((density, dens), (forage, fora), (land, ocean), (diffusivity, diff), (drift, drif))

    def copies(p):
        part = pl.ds(p * PART, PART)
        found = []
        for i, (src, dst) in enumerate(pairs):
            at = (slice(None), part, slice(None)) if len(src.shape) == 3 else (part, slice(None))
            found.append(pltpu.make_async_copy(src.at[at], dst.at[at], sems.at[p, i]))
        return found

    small = [
        pltpu.make_async_copy(src, dst, small_sems.at[i])
        for i, (src, dst) in enumerate(((access_in, access), (mortality_in, mortality), (maturity_in, maturity)))
    ]
    for copy in small:
        copy.start()
    for p in range(PARTS):
        for copy in copies(p):
            copy.start()
    for copy in small:
        copy.wait()
    decay = [jnp.exp(jnp.full((ROWS, BLK), -mortality[c], jnp.float32)) for c in range(last + 1)]

    for p in range(PARTS):
        for copy in copies(p):
            copy.wait()

        def step(i, carry, p=p):
            tiles_at = [p * (PART // ROWS) + i * STEP + t for t in range(STEP)]
            ats = [pl.ds(pl.multiple_of(b * ROWS, ROWS), ROWS) for b in tiles_at]
            rows = [pl.ds(b, ROWS, stride=NB) for b in tiles_at]
            masks = [ocean[at, :].astype(jnp.float32) for at in ats]
            groups = [[fora[g, at, :] for at in ats] for g in range(fora.shape[0])]
            spawned = [maturity[0] * dens[0, at, :] for at in ats]
            for c in range(last + 1):
                weights = [access[g, c] for g in range(len(groups))]
                for t, at in enumerate(ats):
                    total = weights[0] * groups[0][t]
                    for g in range(1, len(groups)):
                        total = total + weights[g] * groups[g][t]
                    habitat = 1.0 / (1.0 + jnp.exp(-total))
                    gain = decay[c] * (0.5 + habitat) * masks[t]
                    if c == 0:
                        gain0[rows[t], :] = gain
                        continue
                    spawned[t] = spawned[t] + maturity[c] * dens[c, at, :]
                    aged = dens[c - 1, at, :]
                    if c == last:
                        aged = aged + flag[0] * dens[last, at, :]
                    if c <= cut:
                        head[c + 1, rows[t], :] = aged * gain
                    else:
                        tail[c - cut - 1, rows[t], :] = aged * gain
            for t, at in enumerate(ats):
                head[0, rows[t], :] = diff[at, :] * masks[t]
                head[1, rows[t], :] = drif[at, :]
                spawn[0, rows[t], :] = spawned[t]
                spawn[1, rows[t], :] = dens[last, at, :]
            return carry

        lax.fori_loop(0, PART // ROWS // STEP, step, 0)


def start_fields(cut, flag, access, mortality, maturity, density, forage, land, diffusivity, drift):
    cohorts = density.shape[0]
    smem = pl.BlockSpec(memory_space=pltpu.SMEM)
    vmem = pl.BlockSpec(memory_space=pltpu.VMEM)
    f32 = jnp.float32
    big = (density, forage, land, diffusivity, drift)
    return pl.pallas_call(
        start_kernel,
        in_specs=[smem] + [pl.BlockSpec(memory_space=pltpu.HBM)] * 8,
        out_specs=[vmem] * 4,
        out_shape=[
            jax.ShapeDtypeStruct((cut + 2, BAND, BLK), f32),
            jax.ShapeDtypeStruct((cohorts - 1 - cut, BAND, BLK), f32),
            jax.ShapeDtypeStruct((BAND, BLK), f32),
            jax.ShapeDtypeStruct((2, BAND, BLK), f32),
        ],
        scratch_shapes=[pltpu.VMEM(a.shape, a.dtype) for a in big]
        + [pltpu.SMEM(a.shape, a.dtype) for a in (access, mortality, maturity)]
        + [pltpu.SemaphoreType.DMA((PARTS, len(big))), pltpu.SemaphoreType.DMA((3,))],
        compiler_params=pltpu.CompilerParams(vmem_limit_bytes=56 * 1024 * 1024),
        cost_estimate=pl.CostEstimate(flops=20 * 16 * BAND * BLK, bytes_accessed=6 * 1024 * 1024, transcendentals=16 * BAND * BLK),
        name="start_fields",
    )(flag, access, mortality, maturity, *big)


def sweep_kernel(group, before, own, after, coef_b, coef_o, coef_a, weights, effort, strata, filled, out, totals, c0, cn, cs, *scratch):
    del filled
    packed, zonal = scratch[:group], scratch[group:]

    @pl.when(pl.program_id(0) == 0)
    def _():
        for i, ref in enumerate((coef_b, coef_o, coef_a)):
            for r in range(ROWS):
                here = pl.ds(r * NB, NB)
                there = pl.ds(i * BAND + r * NB, NB)
                dm = ref[0, here, :]
                half = 0.5 * ref[1, here, :]
                ocean = jnp.where(dm > 0.0, 1.0, 0.0)
                c0[there, :] = ocean - 2.0 * dm
                cn[there, :] = dm - half * ocean
                cs[there, :] = dm + half * ocean

    def put(g, at, x):
        hi, lo = split16(x)
        packed[g][at, :BLK] = hi
        packed[g][at, BLK:] = lo

    def zonal_step(g, k):
        first = (k - 1) * NB
        count = (3 * ROWS + 2 - 2 * k) * NB
        both = jnp.dot(packed[g][first : first + count, :], weights[g], preferred_element_type=jnp.float32)
        zonal[g][first : first + count, :] = both[:, :BLK] + both[:, BLK:]

    def meridional_step(g, k):
        for half in range(NB // 16):
            def rows(r):
                return pl.ds(r * NB + 16 * half, 16)

            south, here = zonal[g][rows(k - 1), :], zonal[g][rows(k), :]
            for r in range(k, 3 * ROWS - k):
                north = zonal[g][rows(r + 1), :]
                field = c0[rows(r), :] * here + cn[rows(r), :] * north + cs[rows(r), :] * south
                south, here = here, north
                if k < SWEEPS:
                    put(g, rows(r), field)
                else:
                    out[g, pl.ds(r - ROWS + 16 * half * ROWS, 16, stride=ROWS), :] = field
                    zonal[g][rows(r - ROWS), :] = field * effort[rows(r - ROWS), :]

    for g in range(group):
        for i, ref in enumerate((before, own, after)):
            for r in range(ROWS):
                put(g, pl.ds(i * BAND + r * NB, NB), ref[g, r * NB : (r + 1) * NB, :])
    for k in range(1, SWEEPS + 1):
        for g in range(group):
            zonal_step(g, k)
            if g > 0:
                meridional_step(g - 1, k)
            elif k > 1 and group > 1:
                meridional_step(group - 1, k - 1)
        if group == 1:
            meridional_step(0, k)
    if group > 1:
        meridional_step(group - 1, SWEEPS)

    for g in range(group):
        sums = [jnp.zeros((8, BLK), jnp.float32) for _ in range(STRATA)]
        for v in range(BAND // 8):
            at = pl.ds(v * 8, 8)
            caught, which = zonal[g][at, :], strata[at, :]
            sums = [sums[s] + jnp.where(which == s, caught, 0.0) for s in range(STRATA)]
        for s in range(STRATA):
            totals[g, s : s + 1, :] = jnp.sum(sums[s], axis=0, keepdims=True)
        totals[g, STRATA:, :] = jnp.zeros((SPAD - STRATA, BLK), jnp.float32)


def sweeps(group, cohorts, offset, first, before, own, after, coefs, weights, effort, strata, filled):
    def blocks(shape, start):
        rest = tuple(pl.Element(n) for n in shape)
        return pl.BlockSpec((pl.Element(group),) + rest, lambda i: (start + group * i, 0, 0))

    own_spec = blocks((BAND, BLK), offset)
    pair = pl.BlockSpec((2, BAND, BLK), lambda i: (0, 0, 0))
    flat = pl.BlockSpec((BAND, BLK), lambda i: (0, 0))
    f32 = jnp.float32
    args = [before, own, after, *coefs, weights, effort, strata]
    in_specs = [own_spec] * 3 + [pair] * 3 + [blocks((2 * BLK, 2 * BLK), first), flat, flat]
    aliases = {}
    if filled is not None:
        args.append(filled)
        in_specs.append(pl.BlockSpec(memory_space=pl.ANY))
        aliases = {len(args) - 1: 0}

    def kernel(*refs):
        refs = list(refs)
        if filled is None:
            refs.insert(9, None)
        sweep_kernel(group, *refs)

    band3 = 3 * BAND
    return pl.pallas_call(
        kernel,
        grid=(cohorts // group,),
        in_specs=in_specs,
        out_specs=[blocks((BAND, BLK), first), pl.BlockSpec((group, SPAD, BLK), lambda i: (i, 0, 0))],
        out_shape=[
            jax.ShapeDtypeStruct((weights.shape[0], BAND, BLK), f32),
            jax.ShapeDtypeStruct((cohorts, SPAD, BLK), f32),
        ],
        scratch_shapes=[pltpu.VMEM((band3, BLK), f32)] * 3
        + [pltpu.VMEM((band3, 2 * BLK), jnp.bfloat16)] * group
        + [pltpu.VMEM((band3, BLK), f32)] * group,
        input_output_aliases=aliases,
        compiler_params=pltpu.CompilerParams(vmem_limit_bytes=32 * 1024 * 1024),
        cost_estimate=pl.CostEstimate(flops=cohorts * 1100 * 1000 * 1000, bytes_accessed=cohorts * 4 * 1024 * 1024, transcendentals=0),
        name="sweeps",
    )(*args)


def tiles(array):
    lead = array.shape[:-2]
    split = array.reshape(lead + (ROWS, NB, BLK))
    return jnp.swapaxes(split, -3, -2).reshape(lead + (BAND, BLK))


def untiles(array):
    lead = array.shape[:-2]
    split = array.reshape(lead + (NB, ROWS, BLK))
    return jnp.swapaxes(split, -3, -2).reshape(lead + (ROWS, NB * BLK))


def by_row(array):
    return array.reshape(BAND, BLK)


def group_sum(table, axes):
    size = 1
    for axis in axes:
        size *= lax.axis_size(axis)
    copies = jnp.broadcast_to(table[None], (size,) + table.shape)
    return jnp.sum(lax.all_to_all(copies, axes, 0, 0, tiled=True), axis=0)


def body(
    density,
    forage,
    access,
    mortality,
    maturity,
    recruit_rate,
    zonal_inverse,
    diffusivity,
    drift,
    land_mask,
    effort,
    strata_map,
    length_bin,
    selectivity,
):
    rank = lax.axis_index(COH)
    ranks = lax.axis_size(COH)
    bands = 128
    up = [(i, i + 1) for i in range(bands - 1)]
    down = [(i + 1, i) for i in range(bands - 1)]

    def halo(array):
        return lax.ppermute(array, LAT, up), lax.ppermute(array, LAT, down)

    is_last = jnp.where(rank == ranks - 1, 1.0, 0.0).reshape(1).astype(jnp.float32)
    cut = 9
    head, tail, gain0, spawn = start_fields(
        cut, is_last, access.T, mortality, maturity, tiles(density), tiles(forage), tiles(land_mask), tiles(diffusivity), tiles(drift)
    )
    head_b, head_a = halo(head)
    onward = jnp.where(rank == ranks - 1, spawn[0], spawn[1])
    ring = lax.ppermute(onward, COH, [(k, (k + 1) % 4) for k in range(4)])
    second = lax.ppermute(spawn[0], COH, [(1, 0)])
    third = lax.ppermute(spawn[0], COH, [(2, 0)])
    tail, head_b, head_a = lax.optimization_barrier((tail, head_b, head_a))
    tail_b, tail_a = halo(tail)

    inverse = jnp.swapaxes(zonal_inverse, 1, 2)
    rounded = lax.reduce_precision(inverse, 8, 7)
    hi, lo = rounded.astype(jnp.bfloat16), (inverse - rounded).astype(jnp.bfloat16)
    weights = jnp.concatenate(
        [jnp.concatenate([hi, lo], axis=2), jnp.concatenate([hi, jnp.zeros_like(lo)], axis=2)], axis=1
    )
    eff, strata, rate = by_row(effort), by_row(strata_map), by_row(recruit_rate)
    coefs = (head_b, head, head_a)
    out, tot1 = sweeps(3, cut, 2, 1, head_b, head, head_a, coefs, weights, eff, strata, None)
    out, ring, second, third = lax.optimization_barrier((out, ring, second, third))
    spawning = spawn[0] + second + third + ring
    recruits = rate * spawning / (1.0 + spawning / 16.0)
    zero = (jnp.where(rank == 0, recruits, ring) * gain0)[None]
    zero_b, zero_a = halo(zero)
    out, tot2 = sweeps(3, 15 - cut, 0, 1 + cut, tail_b, tail, tail_a, coefs, weights, eff, strata, out)
    out, tot0 = sweeps(1, 1, 0, 0, zero_b, zero, zero_a, coefs, weights, eff, strata, out)
    new_density = untiles(out)

    totals = jnp.sum(jnp.concatenate([tot0, tot1, tot2], axis=0), axis=2)
    length_hot = (length_bin[:, None] == jnp.arange(NLEN, dtype=jnp.int32)[None, :]).astype(jnp.float32)
    scaled = length_hot * (selectivity * (25.0 / (1024 * 4096)))[None, :]
    partial_catch = jnp.sum(totals[:, :, None] * scaled[:, None, :], axis=0).reshape(ROWS, BLK)
    table = group_sum(partial_catch, ("x", "y", "core"))
    table = group_sum(table, ("zl", "zh"))
    catch_table = table.reshape(SPAD, NLEN)[:STRATA]
    return (new_density, catch_table)


def solution(mesh):
    grid = Mesh(mesh.devices.reshape([size for _, size in AXES]), [name for name, _ in AXES])
    in_specs = (
        P(COH, LAT, None),
        P(None, LAT, None),
        P(COH, None),
        P(COH),
        P(COH),
        P(LAT, None),
        P(COH, None, None),
        P(LAT, None),
        P(LAT, None),
        P(LAT, None),
        P(LAT, None),
        P(LAT, None),
        P(COH),
        P(),
    )
    out_specs = (P(COH, LAT, None), P())
    return jax.shard_map(body, mesh=grid, in_specs=in_specs, out_specs=out_specs, check_vma=False)
```

```python
import jax
import jax.numpy as jnp
from jax import lax
from jax.experimental import pallas as pl
from jax.experimental.pallas import tpu as pltpu
from jax.sharding import Mesh, PartitionSpec as P

STRATA = 25
NLEN = 32
BLK = 128
SWEEPS = 8
LAT = ("zl", "x", "y", "core")
COH = "zh"
AXES = (("zl", 4), ("x", 4), ("y", 4), ("core", 2), ("zh", 4))
ROWS = 8
NB = 32
BAND = ROWS * NB
SPAD = 32
PARTS = 2
PART = BAND // PARTS
STEP = 4
VMEM = 56 * 1024 * 1024


def split16(x):
    hi = x.astype(jnp.bfloat16)
    lo = (x - hi.astype(jnp.float32)).astype(jnp.bfloat16)
    return hi, lo


def spawn_kernel(flag, maturity, density, spawn, onward):
    part = pl.program_id(0)
    last = density.shape[0] - 1
    for t in range(PART // ROWS):
        at = pl.ds(t * ROWS, ROWS)
        rows = pl.ds(part * (PART // ROWS) + t, ROWS, stride=NB)
        spawned = maturity[0] * density[0, at, :]
        for c in range(1, last + 1):
            spawned = spawned + maturity[c] * density[c, at, :]
        spawn[rows, :] = spawned
        onward[rows, :] = jnp.where(flag[0] > 0.0, spawned, density[last, at, :])


def local_spawn(flag, maturity, density):
    smem = pl.BlockSpec(memory_space=pltpu.SMEM)
    flat = pl.BlockSpec((BAND, BLK), lambda p: (0, 0))
    return pl.pallas_call(
        spawn_kernel,
        grid=(PARTS,),
        in_specs=[smem, smem, pl.BlockSpec((density.shape[0], PART, BLK), lambda p: (0, p, 0))],
        out_specs=[flat, flat],
        out_shape=[jax.ShapeDtypeStruct((BAND, BLK), jnp.float32)] * 2,
        compiler_params=pltpu.CompilerParams(vmem_limit_bytes=VMEM),
        cost_estimate=pl.CostEstimate(flops=32 * BAND * BLK, bytes_accessed=3 * 1024 * 1024, transcendentals=0),
        name="local_spawn",
    )(flag, maturity, density)


def start_kernel(first, count, flag, access, mortality, density, forage, land, *refs):
    part = pl.program_id(0)
    groups = forage.shape[0]
    last = density.shape[0] - 1
    out = refs[-1]
    lead = out.shape[0] - count
    for t in range(0, PART // ROWS, STEP):
        ats = [pl.ds((t + i) * ROWS, ROWS) for i in range(STEP)]
        rows = [pl.ds(part * (PART // ROWS) + t + i, ROWS, stride=NB) for i in range(STEP)]
        ocean = [land[at, :].astype(jnp.float32) for at in ats]
        food = [[forage[g, at, :] for at in ats] for g in range(groups)]
        if lead:
            for i in range(STEP):
                out[0, rows[i], :] = refs[0][ats[i], :] * ocean[i]
                out[1, rows[i], :] = refs[1][ats[i], :]
        for j in range(count):
            c = first + j
            weights = [0.5 * access[g, c] for g in range(groups)]
            decay = jnp.exp(jnp.full((ROWS, BLK), -mortality[c], jnp.float32))
            for i, at in enumerate(ats):
                total = weights[0] * food[0][i]
                for g in range(1, groups):
                    total = total + weights[g] * food[g][i]
                gain = decay * ocean[i] * (1.0 + 0.5 * jnp.tanh(total))
                if c > 0:
                    aged = density[c - 1, at, :]
                    if c == last:
                        aged = aged + flag[0] * density[last, at, :]
                    gain = aged * gain
                out[lead + j, rows[i], :] = gain


def start_fields(first, count, flag, access, mortality, density, forage, land, *coefficients):
    smem = pl.BlockSpec(memory_space=pltpu.SMEM)
    flat = pl.BlockSpec((PART, BLK), lambda p: (p, 0))

    def kernel(*refs):
        start_kernel(first, count, *refs)

    shape = (count + len(coefficients), BAND, BLK)
    return pl.pallas_call(
        kernel,
        grid=(PARTS,),
        in_specs=[
            smem,
            smem,
            smem,
            pl.BlockSpec((density.shape[0], PART, BLK), lambda p: (0, p, 0)),
            pl.BlockSpec((forage.shape[0], PART, BLK), lambda p: (0, p, 0)),
        ]
        + [flat] * (1 + len(coefficients)),
        out_specs=pl.BlockSpec(shape, lambda p: (0, 0, 0)),
        out_shape=jax.ShapeDtypeStruct(shape, jnp.float32),
        compiler_params=pltpu.CompilerParams(vmem_limit_bytes=VMEM),
        cost_estimate=pl.CostEstimate(flops=20 * count * BAND * BLK, bytes_accessed=4 * 1024 * 1024, transcendentals=count * BAND * BLK),
        name="start_fields",
    )(flag, access, mortality, density, forage, land, *coefficients)


def sweep_kernel(group, before, own, after, coef_b, coef_o, coef_a, weights, effort, strata, filled, out, totals, c0, cn, cs, *scratch):
    del filled
    packed, zonal = scratch[:group], scratch[group:]

    @pl.when(pl.program_id(0) == 0)
    def _():
        for i, ref in enumerate((coef_b, coef_o, coef_a)):
            for r in range(ROWS):
                here = pl.ds(r * NB, NB)
                there = pl.ds(i * BAND + r * NB, NB)
                dm = ref[0, here, :]
                half = 0.5 * ref[1, here, :]
                ocean = jnp.where(dm > 0.0, 1.0, 0.0)
                c0[there, :] = ocean - 2.0 * dm
                cn[there, :] = dm - half * ocean
                cs[there, :] = dm + half * ocean

    def put(g, at, x):
        hi, lo = split16(x)
        packed[g][at, :BLK] = hi
        packed[g][at, BLK:] = lo

    def zonal_step(g, k):
        first = (k - 1) * NB
        count = (3 * ROWS + 2 - 2 * k) * NB
        both = jnp.dot(packed[g][first : first + count, :], weights[g], preferred_element_type=jnp.float32)
        zonal[g][first : first + count, :] = both[:, :BLK] + both[:, BLK:]

    def meridional_step(g, k):
        for half in range(NB // 16):
            def rows(r):
                return pl.ds(r * NB + 16 * half, 16)

            south, here = zonal[g][rows(k - 1), :], zonal[g][rows(k), :]
            for r in range(k, 3 * ROWS - k):
                north = zonal[g][rows(r + 1), :]
                field = c0[rows(r), :] * here + cn[rows(r), :] * north + cs[rows(r), :] * south
                south, here = here, north
                if k < SWEEPS:
                    put(g, rows(r), field)
                else:
                    out[g, pl.ds(r - ROWS + 16 * half * ROWS, 16, stride=ROWS), :] = field
                    zonal[g][rows(r - ROWS), :] = field * effort[rows(r - ROWS), :]

    for g in range(group):
        for i, ref in enumerate((before, own, after)):
            for r in range(ROWS):
                put(g, pl.ds(i * BAND + r * NB, NB), ref[g, r * NB : (r + 1) * NB, :])
    for k in range(1, SWEEPS + 1):
        for g in range(group):
            zonal_step(g, k)
            if g > 0:
                meridional_step(g - 1, k)
            elif k > 1 and group > 1:
                meridional_step(group - 1, k - 1)
        if group == 1:
            meridional_step(0, k)
    if group > 1:
        meridional_step(group - 1, SWEEPS)

    for some in (range(0, 13), range(13, STRATA)):
        sums = {(s, g): None for s in some for g in range(group)}
        for v in range(BAND // 8):
            at = pl.ds(v * 8, 8)
            which = strata[at, :]
            caught = [zonal[g][at, :] for g in range(group)]
            for s in some:
                inside = which == s
                for g in range(group):
                    term = jnp.where(inside, caught[g], 0.0)
                    sums[s, g] = term if v == 0 else sums[s, g] + term
        for s in some:
            for g in range(group):
                totals[g, s : s + 1, :] = jnp.sum(sums[s, g], axis=0, keepdims=True)
    for g in range(group):
        totals[g, STRATA:, :] = jnp.zeros((SPAD - STRATA, BLK), jnp.float32)


def sweeps(group, cohorts, offset, first, before, own, after, coefs, weights, effort, strata, filled):
    def blocks(shape, start):
        if start % group:
            return pl.BlockSpec((pl.Element(group),) + tuple(pl.Element(n) for n in shape), lambda i: (start + group * i, 0, 0))
        return pl.BlockSpec((group,) + shape, lambda i: (start // group + i, 0, 0))

    own_spec = blocks((BAND, BLK), offset)
    pair = pl.BlockSpec((2, BAND, BLK), lambda i: (0, 0, 0))
    flat = pl.BlockSpec((BAND, BLK), lambda i: (0, 0))
    f32 = jnp.float32
    args = [before, own, after, *coefs, weights, effort, strata]
    in_specs = [own_spec] * 3 + [pair] * 3 + [blocks((2 * BLK, 2 * BLK), first), flat, flat]
    aliases = {}
    if filled is not None:
        args.append(filled)
        in_specs.append(pl.BlockSpec(memory_space=pl.ANY))
        aliases = {len(args) - 1: 0}

    def kernel(*refs):
        refs = list(refs)
        if filled is None:
            refs.insert(9, None)
        sweep_kernel(group, *refs)

    band3 = 3 * BAND
    return pl.pallas_call(
        kernel,
        grid=(cohorts // group,),
        in_specs=in_specs,
        out_specs=[blocks((BAND, BLK), first), pl.BlockSpec((group, SPAD, BLK), lambda i: (i, 0, 0))],
        out_shape=[
            jax.ShapeDtypeStruct((weights.shape[0], BAND, BLK), f32),
            jax.ShapeDtypeStruct((cohorts, SPAD, BLK), f32),
        ],
        scratch_shapes=[pltpu.VMEM((band3, BLK), f32)] * 3
        + [pltpu.VMEM((band3, 2 * BLK), jnp.bfloat16)] * group
        + [pltpu.VMEM((band3, BLK), f32)] * group,
        input_output_aliases=aliases,
        compiler_params=pltpu.CompilerParams(vmem_limit_bytes=32 * 1024 * 1024),
        cost_estimate=pl.CostEstimate(flops=cohorts * 1100 * 1000 * 1000, bytes_accessed=cohorts * 4 * 1024 * 1024, transcendentals=0),
        name="sweeps",
    )(*args)


def tiles(array):
    lead = array.shape[:-2]
    split = array.reshape(lead + (ROWS, NB, BLK))
    return jnp.swapaxes(split, -3, -2).reshape(lead + (BAND, BLK))


def untiles(array):
    lead = array.shape[:-2]
    split = array.reshape(lead + (NB, ROWS, BLK))
    return jnp.swapaxes(split, -3, -2).reshape(lead + (ROWS, NB * BLK))


def by_row(array):
    return array.reshape(BAND, BLK)


def group_sum(table, axes):
    size = 1
    for axis in axes:
        size *= lax.axis_size(axis)
    copies = jnp.broadcast_to(table[None], (size,) + table.shape)
    return jnp.sum(lax.all_to_all(copies, axes, 0, 0, tiled=True), axis=0)


def body(
    density,
    forage,
    access,
    mortality,
    maturity,
    recruit_rate,
    zonal_inverse,
    diffusivity,
    drift,
    land_mask,
    effort,
    strata_map,
    length_bin,
    selectivity,
):
    rank = lax.axis_index(COH)
    ranks = lax.axis_size(COH)
    bands = 128
    up = [(i, i + 1) for i in range(bands - 1)]
    down = [(i + 1, i) for i in range(bands - 1)]

    def halo(array):
        return lax.ppermute(array, LAT, up), lax.ppermute(array, LAT, down)

    is_last = jnp.where(rank == ranks - 1, 1.0, 0.0).reshape(1).astype(jnp.float32)
    cut = 8
    dense, food, land = tiles(density), tiles(forage), tiles(land_mask)
    spawn, onward = local_spawn(is_last, maturity, dense)
    ring = lax.ppermute(onward, COH, [(k, (k + 1) % 4) for k in range(4)])
    second = lax.ppermute(spawn, COH, [(1, 0)])
    third = lax.ppermute(spawn, COH, [(2, 0)])
    head = start_fields(cut, 16 - cut, is_last, access.T, mortality, dense, food, land, tiles(diffusivity), tiles(drift))
    head_b, head_a = halo(head)
    head_here, dense, food = lax.optimization_barrier((head, dense, food))
    tail = start_fields(0, cut, is_last, access.T, mortality, dense, food, land)
    rate = by_row(recruit_rate)
    spawning = spawn + second + third + ring
    recruits = rate * spawning / (1.0 + spawning / 16.0)
    zero = jnp.where(rank == 0, recruits, ring) * tail[0]
    tail = lax.dynamic_update_slice(tail, zero[None], (0, 0, 0))
    tail_b, tail_a = halo(tail)

    inverse = jnp.swapaxes(zonal_inverse, 1, 2)
    rounded = lax.reduce_precision(inverse, 8, 7)
    hi, lo = rounded.astype(jnp.bfloat16), (inverse - rounded).astype(jnp.bfloat16)
    weights = jnp.concatenate(
        [jnp.concatenate([hi, lo], axis=2), jnp.concatenate([hi, jnp.zeros_like(lo)], axis=2)], axis=1
    )
    eff, strata = by_row(effort), by_row(strata_map)
    coefs = (head_b, head_here, head_a)
    out, tot1 = sweeps(4, 16 - cut, 2, cut, head_b, head_here, head_a, coefs, weights, eff, strata, None)
    out, tot0 = sweeps(4, cut, 0, 0, tail_b, tail, tail_a, coefs, weights, eff, strata, out)
    new_density = untiles(out)

    totals = jnp.sum(jnp.concatenate([tot0, tot1], axis=0), axis=2)
    length_hot = (length_bin[:, None] == jnp.arange(NLEN, dtype=jnp.int32)[None, :]).astype(jnp.float32)
    scaled = length_hot * (selectivity * (25.0 / (1024 * 4096)))[None, :]
    partial_catch = jnp.sum(totals[:, :, None] * scaled[:, None, :], axis=0).reshape(ROWS, BLK)
    table = group_sum(partial_catch, ("x", "y", "core"))
    table = group_sum(table, ("zl", "zh"))
    catch_table = table.reshape(SPAD, NLEN)[:STRATA]
    return (new_density, catch_table)


def solution(mesh):
    grid = Mesh(mesh.devices.reshape([size for _, size in AXES]), [name for name, _ in AXES])
    in_specs = (
        P(COH, LAT, None),
        P(None, LAT, None),
        P(COH, None),
        P(COH),
        P(COH),
        P(LAT, None),
        P(COH, None, None),
        P(LAT, None),
        P(LAT, None),
        P(LAT, None),
        P(LAT, None),
        P(LAT, None),
        P(COH),
        P(),
    )
    out_specs = (P(COH, LAT, None), P())
    return jax.shard_map(body, mesh=grid, in_specs=in_specs, out_specs=out_specs, check_vma=False)
```

```python
import jax
import jax.numpy as jnp
from jax import lax
from jax.experimental import pallas as pl
from jax.experimental.pallas import tpu as pltpu
from jax.sharding import Mesh, PartitionSpec as P

STRATA = 25
NLEN = 32
BLK = 128
SWEEPS = 8
LAT = ("zl", "x", "y", "core")
COH = "zh"
AXES = (("zl", 4), ("x", 4), ("y", 4), ("core", 2), ("zh", 4))
ROWS = 8
NB = 32
BAND = ROWS * NB
SPAD = 32
PARTS = 2
PART = BAND // PARTS
STEP = 4
VMEM = 56 * 1024 * 1024


def split16(x):
    hi = x.astype(jnp.bfloat16)
    lo = (x - hi.astype(jnp.float32)).astype(jnp.bfloat16)
    return hi, lo


def spawn_kernel(flag, maturity, density, spawn, onward):
    part = pl.program_id(0)
    last = density.shape[0] - 1
    for t in range(PART // ROWS):
        at = pl.ds(t * ROWS, ROWS)
        rows = pl.ds(part * (PART // ROWS) + t, ROWS, stride=NB)
        spawned = maturity[0] * density[0, at, :]
        for c in range(1, last + 1):
            spawned = spawned + maturity[c] * density[c, at, :]
        spawn[rows, :] = spawned
        onward[rows, :] = jnp.where(flag[0] > 0.0, spawned, density[last, at, :])


def local_spawn(flag, maturity, density):
    smem = pl.BlockSpec(memory_space=pltpu.SMEM)
    flat = pl.BlockSpec((BAND, BLK), lambda p: (0, 0))
    return pl.pallas_call(
        spawn_kernel,
        grid=(PARTS,),
        in_specs=[smem, smem, pl.BlockSpec((density.shape[0], PART, BLK), lambda p: (0, p, 0))],
        out_specs=[flat, flat],
        out_shape=[jax.ShapeDtypeStruct((BAND, BLK), jnp.float32)] * 2,
        compiler_params=pltpu.CompilerParams(vmem_limit_bytes=VMEM),
        cost_estimate=pl.CostEstimate(flops=32 * BAND * BLK, bytes_accessed=3 * 1024 * 1024, transcendentals=0),
        name="local_spawn",
    )(flag, maturity, density)


def start_kernel(first, count, flag, access, mortality, before, density, forage, land, *refs):
    part = pl.program_id(0)
    groups = forage.shape[0]
    last = access.shape[1] - 1
    out = refs[-1]
    lead = out.shape[0] - count
    for t in range(0, PART // ROWS, STEP):
        ats = [pl.ds((t + i) * ROWS, ROWS) for i in range(STEP)]
        rows = [pl.ds(part * (PART // ROWS) + t + i, ROWS, stride=NB) for i in range(STEP)]
        ocean = [land[at, :].astype(jnp.float32) for at in ats]
        food = [[forage[g, at, :] for at in ats] for g in range(groups)]
        if lead:
            for i in range(STEP):
                out[0, rows[i], :] = refs[0][ats[i], :] * ocean[i]
                out[1, rows[i], :] = refs[1][ats[i], :]
        for j in range(count):
            c = first + j
            weights = [0.5 * access[g, c] for g in range(groups)]
            decay = jnp.exp(jnp.full((ROWS, BLK), -mortality[c], jnp.float32))
            for i, at in enumerate(ats):
                total = weights[0] * food[0][i]
                for g in range(1, groups):
                    total = total + weights[g] * food[g][i]
                gain = decay * ocean[i] * (1.0 + 0.5 * jnp.tanh(total))
                if c > 0:
                    aged = before[0, at, :] if j == 0 else density[j - 1, at, :]
                    if c == last:
                        aged = aged + flag[0] * density[j, at, :]
                    gain = aged * gain
                out[lead + j, rows[i], :] = gain


def start_fields(first, count, flag, access, mortality, density, forage, land, *coefficients):
    smem = pl.BlockSpec(memory_space=pltpu.SMEM)
    flat = pl.BlockSpec((PART, BLK), lambda p: (p, 0))

    def kernel(*refs):
        start_kernel(first, count, *refs)

    shape = (count + len(coefficients), BAND, BLK)
    return pl.pallas_call(
        kernel,
        grid=(PARTS,),
        in_specs=[
            smem,
            smem,
            smem,
            pl.BlockSpec((1, PART, BLK), lambda p: (max(first - 1, 0), p, 0)),
            pl.BlockSpec((count, PART, BLK), lambda p: (first // count, p, 0)),
            pl.BlockSpec((forage.shape[0], PART, BLK), lambda p: (0, p, 0)),
        ]
        + [flat] * (1 + len(coefficients)),
        out_specs=pl.BlockSpec(shape, lambda p: (0, 0, 0)),
        out_shape=jax.ShapeDtypeStruct(shape, jnp.float32),
        compiler_params=pltpu.CompilerParams(vmem_limit_bytes=VMEM),
        cost_estimate=pl.CostEstimate(flops=20 * count * BAND * BLK, bytes_accessed=4 * 1024 * 1024, transcendentals=count * BAND * BLK),
        name="start_fields",
    )(flag, access, mortality, density, density, forage, land, *coefficients)


def sweep_kernel(group, before, own, after, coef_b, coef_o, coef_a, weights, effort, strata, filled, out, totals, c0, cn, cs, *scratch):
    del filled
    packed, zonal = scratch[:group], scratch[group:]

    @pl.when(pl.program_id(0) == 0)
    def _():
        for i, ref in enumerate((coef_b, coef_o, coef_a)):
            for r in range(ROWS):
                here = pl.ds(r * NB, NB)
                there = pl.ds(i * BAND + r * NB, NB)
                dm = ref[0, here, :]
                half = 0.5 * ref[1, here, :]
                ocean = jnp.where(dm > 0.0, 1.0, 0.0)
                c0[there, :] = ocean - 2.0 * dm
                cn[there, :] = dm - half * ocean
                cs[there, :] = dm + half * ocean

    def put(g, at, x):
        hi, lo = split16(x)
        packed[g][at, :BLK] = hi
        packed[g][at, BLK:] = lo

    def zonal_step(g, k):
        first = (k - 1) * NB
        count = (3 * ROWS + 2 - 2 * k) * NB
        both = jnp.dot(packed[g][first : first + count, :], weights[g], preferred_element_type=jnp.float32)
        zonal[g][first : first + count, :] = both[:, :BLK] + both[:, BLK:]

    def meridional_step(g, k):
        for half in range(NB // 16):
            def rows(r):
                return pl.ds(r * NB + 16 * half, 16)

            south, here = zonal[g][rows(k - 1), :], zonal[g][rows(k), :]
            for r in range(k, 3 * ROWS - k):
                north = zonal[g][rows(r + 1), :]
                field = c0[rows(r), :] * here + cn[rows(r), :] * north + cs[rows(r), :] * south
                south, here = here, north
                if k < SWEEPS:
                    put(g, rows(r), field)
                else:
                    out[g, pl.ds(r - ROWS + 16 * half * ROWS, 16, stride=ROWS), :] = field
                    zonal[g][rows(r - ROWS), :] = field * effort[rows(r - ROWS), :]

    for g in range(group):
        for i, ref in enumerate((before, own, after)):
            for r in range(ROWS):
                put(g, pl.ds(i * BAND + r * NB, NB), ref[g, r * NB : (r + 1) * NB, :])
    for k in range(1, SWEEPS + 1):
        for g in range(group):
            zonal_step(g, k)
            if g > 0:
                meridional_step(g - 1, k)
            elif k > 1 and group > 1:
                meridional_step(group - 1, k - 1)
        if group == 1:
            meridional_step(0, k)
    if group > 1:
        meridional_step(group - 1, SWEEPS)

    for some in (range(0, 13), range(13, STRATA)):
        sums = {(s, g): None for s in some for g in range(group)}
        for v in range(BAND // 8):
            at = pl.ds(v * 8, 8)
            which = strata[at, :]
            caught = [zonal[g][at, :] for g in range(group)]
            for s in some:
                inside = which == s
                for g in range(group):
                    term = jnp.where(inside, caught[g], 0.0)
                    sums[s, g] = term if v == 0 else sums[s, g] + term
        for s in some:
            for g in range(group):
                totals[g, s : s + 1, :] = jnp.sum(sums[s, g], axis=0, keepdims=True)
    for g in range(group):
        totals[g, STRATA:, :] = jnp.zeros((SPAD - STRATA, BLK), jnp.float32)


def sweeps(group, cohorts, offset, first, before, own, after, coefs, weights, effort, strata, filled):
    def blocks(shape, start):
        if start % group:
            return pl.BlockSpec((pl.Element(group),) + tuple(pl.Element(n) for n in shape), lambda i: (start + group * i, 0, 0))
        return pl.BlockSpec((group,) + shape, lambda i: (start // group + i, 0, 0))

    own_spec = blocks((BAND, BLK), offset)
    pair = pl.BlockSpec((2, BAND, BLK), lambda i: (0, 0, 0))
    flat = pl.BlockSpec((BAND, BLK), lambda i: (0, 0))
    f32 = jnp.float32
    args = [before, own, after, *coefs, weights, effort, strata]
    in_specs = [own_spec] * 3 + [pair] * 3 + [blocks((2 * BLK, 2 * BLK), first), flat, flat]
    aliases = {}
    if filled is not None:
        args.append(filled)
        in_specs.append(pl.BlockSpec(memory_space=pl.ANY))
        aliases = {len(args) - 1: 0}

    def kernel(*refs):
        refs = list(refs)
        if filled is None:
            refs.insert(9, None)
        sweep_kernel(group, *refs)

    band3 = 3 * BAND
    return pl.pallas_call(
        kernel,
        grid=(cohorts // group,),
        in_specs=in_specs,
        out_specs=[blocks((BAND, BLK), first), pl.BlockSpec((group, SPAD, BLK), lambda i: (i, 0, 0))],
        out_shape=[
            jax.ShapeDtypeStruct((weights.shape[0], BAND, BLK), f32),
            jax.ShapeDtypeStruct((cohorts, SPAD, BLK), f32),
        ],
        scratch_shapes=[pltpu.VMEM((band3, BLK), f32)] * 3
        + [pltpu.VMEM((band3, 2 * BLK), jnp.bfloat16)] * group
        + [pltpu.VMEM((band3, BLK), f32)] * group,
        input_output_aliases=aliases,
        compiler_params=pltpu.CompilerParams(vmem_limit_bytes=32 * 1024 * 1024),
        cost_estimate=pl.CostEstimate(flops=cohorts * 1100 * 1000 * 1000, bytes_accessed=cohorts * 4 * 1024 * 1024, transcendentals=0),
        name="sweeps",
    )(*args)


def tiles(array):
    lead = array.shape[:-2]
    split = array.reshape(lead + (ROWS, NB, BLK))
    return jnp.swapaxes(split, -3, -2).reshape(lead + (BAND, BLK))


def untiles(array):
    lead = array.shape[:-2]
    split = array.reshape(lead + (NB, ROWS, BLK))
    return jnp.swapaxes(split, -3, -2).reshape(lead + (ROWS, NB * BLK))


def by_row(array):
    return array.reshape(BAND, BLK)


def group_sum(table, axes):
    size = 1
    for axis in axes:
        size *= lax.axis_size(axis)
    copies = jnp.broadcast_to(table[None], (size,) + table.shape)
    return jnp.sum(lax.all_to_all(copies, axes, 0, 0, tiled=True), axis=0)


def body(
    density,
    forage,
    access,
    mortality,
    maturity,
    recruit_rate,
    zonal_inverse,
    diffusivity,
    drift,
    land_mask,
    effort,
    strata_map,
    length_bin,
    selectivity,
):
    rank = lax.axis_index(COH)
    ranks = lax.axis_size(COH)
    bands = 128
    up = [(i, i + 1) for i in range(bands - 1)]
    down = [(i + 1, i) for i in range(bands - 1)]

    def halo(array):
        return lax.ppermute(array, LAT, up), lax.ppermute(array, LAT, down)

    is_last = jnp.where(rank == ranks - 1, 1.0, 0.0).reshape(1).astype(jnp.float32)
    cut = 8
    dense, food, land = tiles(density), tiles(forage), tiles(land_mask)
    spawn, onward = local_spawn(is_last, maturity, dense)
    ring = lax.ppermute(onward, COH, [(k, (k + 1) % 4) for k in range(4)])
    second = lax.ppermute(spawn, COH, [(1, 0)])
    third = lax.ppermute(spawn, COH, [(2, 0)])
    head = start_fields(cut, 16 - cut, is_last, access.T, mortality, dense, food, land, tiles(diffusivity), tiles(drift))
    head_b, head_a = halo(head)
    head_here, dense, food = lax.optimization_barrier((head, dense, food))
    tail = start_fields(0, cut, is_last, access.T, mortality, dense, food, land)
    rate = by_row(recruit_rate)
    spawning = spawn + second + third + ring
    recruits = rate * spawning / (1.0 + spawning / 16.0)
    zero = jnp.where(rank == 0, recruits, ring) * tail[0]
    tail = lax.dynamic_update_slice(tail, zero[None], (0, 0, 0))
    tail_b, tail_a = halo(tail)

    inverse = jnp.swapaxes(zonal_inverse, 1, 2)
    rounded = lax.reduce_precision(inverse, 8, 7)
    hi, lo = rounded.astype(jnp.bfloat16), (inverse - rounded).astype(jnp.bfloat16)
    weights = jnp.concatenate(
        [jnp.concatenate([hi, lo], axis=2), jnp.concatenate([hi, jnp.zeros_like(lo)], axis=2)], axis=1
    )
    eff, strata = by_row(effort), by_row(strata_map)
    coefs = (head_b, head_here, head_a)
    out, tot1 = sweeps(4, 16 - cut, 2, cut, head_b, head_here, head_a, coefs, weights, eff, strata, None)
    out, tot0 = sweeps(4, cut, 0, 0, tail_b, tail, tail_a, coefs, weights, eff, strata, out)
    new_density = untiles(out)

    totals = jnp.sum(jnp.concatenate([tot0, tot1], axis=0), axis=2)
    length_hot = (length_bin[:, None] == jnp.arange(NLEN, dtype=jnp.int32)[None, :]).astype(jnp.float32)
    scaled = length_hot * (selectivity * (25.0 / (1024 * 4096)))[None, :]
    partial_catch = jnp.sum(totals[:, :, None] * scaled[:, None, :], axis=0).reshape(ROWS, BLK)
    table = group_sum(partial_catch, ("x", "y", "core"))
    table = group_sum(table, ("zl", "zh"))
    catch_table = table.reshape(SPAD, NLEN)[:STRATA]
    return (new_density, catch_table)


def solution(mesh):
    grid = Mesh(mesh.devices.reshape([size for _, size in AXES]), [name for name, _ in AXES])
    in_specs = (
        P(COH, LAT, None),
        P(None, LAT, None),
        P(COH, None),
        P(COH),
        P(COH),
        P(LAT, None),
        P(COH, None, None),
        P(LAT, None),
        P(LAT, None),
        P(LAT, None),
        P(LAT, None),
        P(LAT, None),
        P(COH),
        P(),
    )
    out_specs = (P(COH, LAT, None), P())
    return jax.shard_map(body, mesh=grid, in_specs=in_specs, out_specs=out_specs, check_vma=False)
```
